32 devices in a mesh: groups: 2 (over y), tensor: 4 (over x, core), pool: 4 (over z).
Axes of the slice: x: 2, y: 2, z: 4, core: 2. Of those that a mesh axis runs over, the one named last changes fastest.
Arguments:
- queries: bfloat16 [1024, 8192], P(('groups', 'tensor'), 'pool'), parts along dimension 0
- key_value_cache: bfloat16 [1024, 128, 2, 1024], P(('groups', 'tensor'), None, None, 'pool'), parts along dimension 0
- cache_lengths: int32 [1024], P(('groups', 'tensor')), parts along dimension 0, may hold values from 1 to 128
- block_adapter_slot: int32 [8], P('groups'), parts along dimension 0, may hold values from 0 to 7, as said below
- output_weight: bfloat16 [8192, 8192], P('pool', 'tensor'), may hold values from -0.0625 to 0.0625
- adapter_down_weight: bfloat16 [16, 8192, 64], P(('groups', 'tensor'), 'pool'), parts along dimension 0, may hold values from -0.0625 to 0.0625
- adapter_up_weight: bfloat16 [16, 64, 8192], P('groups', 'pool', 'tensor'), parts along dimension 0, may hold values from -0.75 to 0.75
Outputs:
- projected: bfloat16 [1024, 8192], P(('groups', 'pool'), 'tensor'), parts along dimension 0
The draws below stay inside these ranges and needn't reach their ends.
There are 2 independent parts, one for each index of `groups`. The reference program is written for one: setup_inputs(seed, part) draws one part's arguments, and reference() takes and returns one part's arrays. A program takes and returns all parts, laid end to end along the dimension named above; an argument that names none is the same for every part. Nothing has to cross between parts.
Inputs may be any that keep to these rules, and one draw needn't show every extreme that they name: `block_adapter_slot`: block b covers rows b * 128 to (b + 1) * 128 - 1. Each run of 2 slots that starts at a multiple of 2 is named by at least one block.
All inputs are finite; a program needn't handle non-finite values.
Results may differ from the reference program's by a relative error of at most 0.0058.
Values may be sent and summed in bfloat16 or wider, within the bound.
A program may use at most 128 MiB of HBM per device.

```python
import math
import jax
import jax.numpy as jnp
from jax import lax

MODEL_WIDTH = 8192
H = 64
KVH = 8
HD = 128
ADAPTER_RANK = 64
BLK = 128
SLOT_DEV = 2
L = 128
ROWS = 512
BLOCKS = 4
ADAPTER_COUNT = 8


def shared_keys(key):
    return jax.random.normal(key, (ROWS, L, KVH * HD), jnp.float32)


def draw_queries(key, part):
    key = jax.random.fold_in(key, 1)
    drawn_rows = jax.random.normal(key, (ROWS, MODEL_WIDTH), jnp.float32)
    return drawn_rows.astype(jnp.bfloat16)


def draw_key_value_cache(key, part):
    key_draw = shared_keys(key)
    key = jax.random.fold_in(key, 2)
    values_drawn = jax.random.normal(key, (ROWS, L, KVH * HD), jnp.float32)
    return jnp.stack([key_draw, values_drawn], axis=2).astype(jnp.bfloat16)


def draw_block_adapter_slot(key, part):
    key = jax.random.fold_in(key, 3)
    key_owner, key_rest, key_offset = jax.random.split(key, 3)
    owner_count = ADAPTER_COUNT // SLOT_DEV
    owners_first = jax.random.permutation(key_owner, owner_count).astype(jnp.int32)
    owners_rest = jax.random.randint(key_rest, (BLOCKS - owner_count,), 0, owner_count, dtype=jnp.int32)
    owners = jnp.concatenate([owners_first, owners_rest])
    offsets = jax.random.randint(key_offset, (BLOCKS,), 0, SLOT_DEV, dtype=jnp.int32)
    leading = jnp.arange(BLOCKS, dtype=jnp.int32) < owner_count
    offsets = jnp.where(leading & (owners == owner_count - 1), SLOT_DEV - 1, offsets)
    offsets = jnp.where(leading & (owners == 0), 0, offsets)
    return (owners * SLOT_DEV + offsets).astype(jnp.int32)


def set_ends(result, own_key, smallest, top_value):
    longest = result.shape.index(max(result.shape))
    spots = []
    for shift in (0, 1):
        where = [jax.random.randint(jax.random.fold_in(own_key, axis), (), 0, length) for axis, length in enumerate(result.shape)]
        where[longest] = (where[longest] + shift) % result.shape[longest]
        spots.append(tuple(where))
    return result.at[spots[0]].set(smallest).at[spots[1]].set(top_value)


def level_of(rng, extent, shards, least, high):
    level = 1.0
    for position, shards_of in shards:
        heights = jax.random.uniform(jax.random.fold_in(jax.random.fold_in(rng, 6), position), (shards_of,), jnp.float32, least / len(shards), high / len(shards))
        level = level * jnp.repeat(jnp.exp(heights), extent[position] // shards_of).reshape((-1,) + (1,) * (len(extent) - 1 - position))
    return level


def noise(stream_key, extent, spread, reach, cuts=(), kind=jnp.bfloat16):
    entries = spread * jax.random.normal(stream_key, extent, jnp.float32)
    if cuts:
        entries = entries * level_of(stream_key, extent, cuts, -0.22, 0.18)
    return jnp.clip(entries, -reach, reach).astype(kind)


def setup_inputs(seed: int = 0, part: int = 0) -> dict:
    key_of = jax.random.split(jax.random.key(seed), 8)
    own_keys = jax.random.split(jax.random.fold_in(key_of[7], part), 8)
    return {
        "queries": draw_queries(jax.random.fold_in(jax.random.fold_in(key_of[7], part), 71), part),
        "key_value_cache": draw_key_value_cache(jax.random.fold_in(jax.random.fold_in(key_of[7], part), 71), part),
        "cache_lengths": set_ends(jax.random.randint(own_keys[2], (ROWS,), 1, L + 1), jax.random.fold_in(own_keys[2], 1), 1, L).astype(jnp.int32),
        "block_adapter_slot": draw_block_adapter_slot(jax.random.fold_in(jax.random.fold_in(key_of[7], part), 71), part),
        "output_weight": noise(key_of[4], (MODEL_WIDTH, MODEL_WIDTH), MODEL_WIDTH ** -0.5, 0.0625, ((0, 4), (1, 4))),
        "adapter_down_weight": noise(own_keys[5], (ADAPTER_COUNT, MODEL_WIDTH, ADAPTER_RANK), MODEL_WIDTH ** -0.5, 0.0625, ((0, 4), (1, 4))),
        "adapter_up_weight": noise(own_keys[6], (ADAPTER_COUNT, ADAPTER_RANK, MODEL_WIDTH), ADAPTER_RANK ** -0.5, 0.75, ((1, 4), (2, 4))),
    }


adapter_scale = 2.0

def attend_rows(pieces):
    query_rows, cache_rows, length_rows = pieces
    row_count = query_rows.shape[0]
    group_size = H // KVH
    q_four = query_rows.astype(jnp.float32).reshape(row_count, KVH, group_size, HD)
    key_rows = cache_rows[:, :, 0].astype(jnp.float32).reshape(row_count, L, KVH, HD)
    value_rows = cache_rows[:, :, 1].astype(jnp.float32).reshape(row_count, L, KVH, HD)
    scores = jnp.einsum('rkgd,rjkd->rkgj', q_four, key_rows) * (1.0 / math.sqrt(HD))
    visible = (jnp.arange(L, dtype=jnp.int32)[None, :] < length_rows[:, None])[:, None, None, :]
    row_max = lax.optimization_barrier(jnp.max(jnp.where(visible, scores, -1e+30), axis=-1))
    expo_terms = jnp.where(visible, jnp.exp(scores - row_max[..., None]), 0.0)
    totals = lax.optimization_barrier(jnp.sum(expo_terms, axis=-1))
    weights = lax.optimization_barrier(expo_terms.astype(jnp.bfloat16))
    mixed_rows = jnp.einsum('rkgj,rjkd->rkgd', weights.astype(jnp.float32), value_rows) / totals[..., None]
    return mixed_rows.reshape(row_count, H * HD).astype(jnp.bfloat16)

def reference(queries, key_value_cache, cache_lengths, block_adapter_slot, output_weight, adapter_down_weight, adapter_up_weight):
    n_blocks = ROWS // BLK
    attended = lax.map(attend_rows, (queries.reshape(n_blocks, BLK, MODEL_WIDTH), key_value_cache.reshape(n_blocks, BLK, L, 2, KVH * HD), cache_lengths.reshape(n_blocks, BLK)))
    attended = attended.reshape(ROWS, MODEL_WIDTH)
    base_output = jnp.dot(attended, output_weight, preferred_element_type=jnp.float32)
    picked_down_weight = jnp.take(adapter_down_weight, block_adapter_slot, axis=0).astype(jnp.float32)
    picked_up_weight = jnp.take(adapter_up_weight, block_adapter_slot, axis=0).astype(jnp.float32)
    shrink = jnp.einsum('bnd,bdr->bnr', attended.reshape(BLOCKS, BLK, MODEL_WIDTH).astype(jnp.float32), picked_down_weight)
    shrink = lax.optimization_barrier(shrink.astype(jnp.bfloat16))
    expand_rows = jnp.einsum('bnr,brd->bnd', shrink.astype(jnp.float32), picked_up_weight).reshape(ROWS, MODEL_WIDTH)
    return (base_output + adapter_scale * expand_rows).astype(jnp.bfloat16)
```

```python
import functools
import math

import jax
import jax.numpy as jnp
from jax import lax
from jax.experimental import pallas as pl
from jax.experimental.pallas import tpu as pltpu
from jax.sharding import PartitionSpec as P

H = 64
KVH = 8
HD = 128
BLK = 128
GROUP = H // KVH

adapter_scale = 2.0


def attend_row(q, kv, length):
    heads = q.shape[0]
    local_kv = heads // GROUP
    owner = lax.broadcasted_iota(jnp.int32, (heads, HD), 0) // GROUP
    wide = jnp.concatenate(
        [jnp.where(owner == k, q, jnp.zeros_like(q)) for k in range(local_kv)], axis=1
    )
    scores = lax.dot_general(
        wide, kv, (((1,), (1,)), ((), ())), preferred_element_type=jnp.float32
    ) * (1.0 / math.sqrt(HD))
    column = lax.broadcasted_iota(jnp.int32, scores.shape, 1)
    visible = (column % 2 == 0) & (column < 2 * length)
    scores = jnp.where(visible, scores, -1e30)
    expo = jnp.where(visible, jnp.exp(scores - jnp.max(scores, axis=1, keepdims=True)), 0.0)
    totals = jnp.sum(expo, axis=1, keepdims=True)
    weights = pltpu.roll(expo, 1, 1).astype(jnp.bfloat16)
    mixed = jnp.dot(weights, kv, preferred_element_type=jnp.float32)
    picked = mixed[:, :HD]
    for k in range(1, local_kv):
        picked = jnp.where(owner == k, mixed[:, k * HD : (k + 1) * HD], picked)
    return (picked / totals).astype(jnp.bfloat16)


def attention_kernel(step_rows, lengths, q_ref, kv_ref, o_ref):
    base = pl.program_id(0) * step_rows
    positions, _, width = kv_ref.shape[1:]
    for r in range(step_rows):
        kv = kv_ref[r].reshape(positions * 2, width)
        o_ref[r] = attend_row(q_ref[r], kv, lengths[base + r])


def local_attention(queries, key_value_cache, cache_lengths):
    rows, width = queries.shape
    heads = width // HD
    positions, _, kv_width = key_value_cache.shape[1:]
    step = 8
    out = pl.pallas_call(
        functools.partial(attention_kernel, step),
        grid_spec=pltpu.PrefetchScalarGridSpec(
            num_scalar_prefetch=1,
            grid=(rows // step,),
            in_specs=[
                pl.BlockSpec((step, heads, HD), lambda i, n: (i, 0, 0)),
                pl.BlockSpec((step, positions, 2, kv_width), lambda i, n: (i, 0, 0, 0)),
            ],
            out_specs=pl.BlockSpec((step, heads, HD), lambda i, n: (i, 0, 0)),
        ),
        out_shape=jax.ShapeDtypeStruct((rows, heads, HD), jnp.bfloat16),
        compiler_params=pltpu.CompilerParams(vmem_limit_bytes=40 * 1024 * 1024),
    )(cache_lengths, queries.reshape(rows, heads, HD), key_value_cache)
    return out.reshape(rows, width)


def local(
    queries,
    key_value_cache,
    cache_lengths,
    block_adapter_slot,
    output_weight,
    adapter_down_weight,
    adapter_up_weight,
):
    attended = local_attention(queries, key_value_cache, cache_lengths)
    row_count, feat_width = attended.shape
    tensor_index = lax.axis_index("tensor")
    per_device = row_count // BLK
    local_slots = lax.dynamic_slice_in_dim(
        block_adapter_slot, tensor_index * per_device, per_device
    )
    slot_range = lax.all_gather(adapter_down_weight, "tensor", axis=0, tiled=True)
    chosen = jnp.take(slot_range, local_slots, axis=0)
    partial_value = jnp.einsum(
        "bnd,bdr->bnr",
        attended.reshape(per_device, BLK, feat_width),
        chosen,
        preferred_element_type=jnp.float32,
    )
    partial_value = partial_value.reshape(row_count, -1)
    rank_share = lax.psum_scatter(partial_value, "pool", scatter_dimension=1, tiled=True).astype(
        jnp.bfloat16
    )
    rank_share_width = adapter_up_weight.shape[1]
    output_columns = adapter_up_weight.shape[2]
    att_piece = lax.all_gather(attended, "tensor", axis=0, tiled=True)
    share_piece = lax.all_gather(rank_share, "tensor", axis=0, tiled=True)
    piece_rows = att_piece.shape[0]
    block_count = piece_rows // BLK
    block_ids = jnp.arange(block_count, dtype=jnp.int32)
    piece_slots = jnp.take(block_adapter_slot, block_ids)
    picked_up = jnp.take(adapter_up_weight, piece_slots, axis=0)
    base_output = jnp.dot(att_piece, output_weight, preferred_element_type=jnp.float32)
    expand_rows = jnp.einsum(
        "bnr,brd->bnd",
        share_piece.reshape(block_count, BLK, rank_share_width),
        picked_up,
        preferred_element_type=jnp.float32,
    )
    expand_rows = expand_rows.reshape(piece_rows, output_columns)
    gathered_rows = base_output + adapter_scale * expand_rows
    return lax.psum_scatter(
        gathered_rows.astype(jnp.bfloat16), "pool", scatter_dimension=0, tiled=True
    )


def solution(mesh):
    in_specs = (
        P(("groups", "tensor"), "pool"),
        P(("groups", "tensor"), None, None, "pool"),
        P(("groups", "tensor")),
        P("groups"),
        P("pool", "tensor"),
        P(("groups", "tensor"), "pool", None),
        P("groups", "pool", "tensor"),
    )
    out_specs = P(("groups", "pool"), "tensor")
    return jax.shard_map(local, mesh=mesh, in_specs=in_specs, out_specs=out_specs, check_vma=False)
```

```python
import functools
import math

import jax
import jax.numpy as jnp
from jax import lax
from jax.experimental import pallas as pl
from jax.experimental.pallas import tpu as pltpu
from jax.sharding import PartitionSpec as P

H = 64
KVH = 8
HD = 128
BLK = 128
GROUP = H // KVH

adapter_scale = 2.0


def attention_kernel(step_rows, lengths, q_ref, kv_ref, o_ref):
    base = pl.program_id(0) * step_rows
    positions, _, width = kv_ref.shape[1:]
    heads = q_ref.shape[1]
    local_kv = heads // GROUP
    owner = lax.broadcasted_iota(jnp.int32, (heads, HD), 0) // GROUP
    column = lax.broadcasted_iota(jnp.int32, (heads, positions * 2), 1)
    rows = range(step_rows)
    caches = [kv_ref[r].reshape(positions * 2, width) for r in rows]
    all_scores = []
    for r in rows:
        q = q_ref[r]
        wide = jnp.concatenate(
            [jnp.where(owner == k, q, jnp.zeros_like(q)) for k in range(local_kv)], axis=1
        )
        all_scores.append(
            lax.dot_general(
                wide, caches[r], (((1,), (1,)), ((), ())), preferred_element_type=jnp.float32
            )
        )
    seen = jnp.concatenate(
        [(column % 2 + jnp.where(column < 2 * lengths[base + r], 0, 2)) for r in rows], axis=0
    )
    visible = seen == 0
    scores = jnp.where(visible, jnp.concatenate(all_scores, axis=0) * (1.0 / math.sqrt(HD)), -1e30)
    expo = jnp.where(visible, jnp.exp(scores - jnp.max(scores, axis=1, keepdims=True)), 0.0)
    totals = jnp.sum(expo, axis=1, keepdims=True)
    weights = pltpu.roll(expo, 1, 1).astype(jnp.bfloat16)
    all_mixed = [
        jnp.dot(
            weights[r * heads : (r + 1) * heads], caches[r], preferred_element_type=jnp.float32
        )
        for r in rows
    ]
    for r in rows:
        mixed = all_mixed[r]
        picked = mixed[:, :HD]
        for k in range(1, local_kv):
            picked = jnp.where(owner == k, mixed[:, k * HD : (k + 1) * HD], picked)
        o_ref[r] = (picked / totals[r * heads : (r + 1) * heads]).astype(jnp.bfloat16)


def local_attention(queries, key_value_cache, cache_lengths):
    rows, width = queries.shape
    heads = width // HD
    positions, _, kv_width = key_value_cache.shape[1:]
    step = 8
    out = pl.pallas_call(
        functools.partial(attention_kernel, step),
        grid_spec=pltpu.PrefetchScalarGridSpec(
            num_scalar_prefetch=1,
            grid=(rows // step,),
            in_specs=[
                pl.BlockSpec((step, heads, HD), lambda i, n: (i, 0, 0)),
                pl.BlockSpec((step, positions, 2, kv_width), lambda i, n: (i, 0, 0, 0)),
            ],
            out_specs=pl.BlockSpec((step, heads, HD), lambda i, n: (i, 0, 0)),
        ),
        out_shape=jax.ShapeDtypeStruct((rows, heads, HD), jnp.bfloat16),
        compiler_params=pltpu.CompilerParams(vmem_limit_bytes=40 * 1024 * 1024),
    )(cache_lengths, queries.reshape(rows, heads, HD), key_value_cache)
    return out.reshape(rows, width)

MESH = pl.DeviceIdType.MESH


def project_kernel(
    nt, np_, chunks,
    att, weight, down, mask, up_mine, out,
    full, total, inbox, outbox, ups, shr, shr_in, shr_sum, shr_peer,
    att_send, att_recv, core_send, core_recv, hop_send, hop_recv,
    up_send, up_recv, one_send, one_recv, two_send, two_recv,
):
    t, p = lax.axis_index("tensor"), lax.axis_index("pool")
    block = att.shape[0]
    rows = full.shape[0]
    share = rows // np_
    wide = weight.shape[1] // chunks
    per_share = share // BLK

    def copy(src, dst, send, recv, **where):
        return pltpu.make_async_remote_copy(
            src_ref=src, dst_ref=dst, send_sem=send, recv_sem=recv,
            device_id=where, device_id_type=MESH,
        )

    def rows_of(index, size):
        return pl.ds(pl.multiple_of(index * size, size), size)

    barrier = pltpu.get_barrier_semaphore()
    for k in range(1, nt):
        pl.semaphore_signal(barrier, 1, device_id={"tensor": (t + k) % nt}, device_id_type=MESH)
    for k in range(1, np_):
        pl.semaphore_signal(barrier, 1, device_id={"pool": (p + k) % np_}, device_id_type=MESH)
    pl.semaphore_wait(barrier, nt + np_ - 2)

    other = t + 1 - 2 * (t % 2)
    own_at = full.at[rows_of(t, block)]
    sends = []
    for k in range(1, nt // 2):
        to = (t + 2 * k) % nt
        sends.append(copy(att, own_at, att_send.at[k], att_recv.at[k], tensor=to))
    sends.append(copy(att, own_at, core_send.at[0], core_recv.at[0], tensor=other))
    for k in range(1, np_):
        q = (p + k) % np_
        sends.append(
            copy(up_mine.at[pl.ds(q * per_share, per_share)], ups.at[k], up_send.at[k], up_recv.at[k], pool=q)
        )
    for each in sends:
        each.start()
    full[rows_of(t, block), :] = att[...]
    for k in range(1, nt // 2):
        came = (t + nt - 2 * k) % nt
        at = full.at[rows_of(came, block)]
        copy(att, at, att_send.at[k], att_recv.at[k], tensor=came).wait_recv()
        relay = copy(at, at, core_send.at[k], core_recv.at[k], tensor=other)
        relay.start()
        sends.append(relay)
    for k in range(nt // 2):
        at = full.at[rows_of((other + nt - 2 * k) % nt, block)]
        copy(att, at, core_send.at[k], core_recv.at[k], tensor=other).wait_recv()

    def shrink(i, carry):
        at = pl.ds(pl.multiple_of(i * BLK, BLK), BLK)
        part = jnp.dot(full[at, :], down[...], preferred_element_type=jnp.float32)
        shr[at, :] = jnp.where(mask[at, :] > 0, part, 0.0).astype(jnp.bfloat16)
        return carry

    def hop(way, q, c):
        to = p + 1 if way == 0 else p - 1
        to = jnp.clip(to, 0, np_ - 1)
        return copy(
            outbox.at[way, q, c], inbox.at[way, q, c],
            hop_send.at[way, q, c], hop_recv.at[way, q, c], pool=to,
        )

    ends = (0, np_ - 1)

    def first_hops(c):
        cols = pl.ds(pl.multiple_of(c * wide, wide), wide)
        for k in range(np_ - 1):
            for way in (0, 1):
                q = np_ - 1 - k if way == 0 else k

                @pl.when(p == ends[way])
                def _():
                    part = total[q * share : (q + 1) * share, cols]
                    outbox[way, q, c] = part.astype(jnp.bfloat16)
                    hop(way, q, c).start()

    def later_hops(c):
        cols = pl.ds(pl.multiple_of(c * wide, wide), wide)
        for k in range(np_ - 1):
            for way in (0, 1):
                q = np_ - 1 - k if way == 0 else k
                ahead = (q > p) if way == 0 else (q < p)

                @pl.when(ahead & (p != ends[way]))
                def _():
                    hop(way, q, c).wait_recv()
                    part = total[q * share : (q + 1) * share, cols]
                    part = part + inbox[way, q, c].astype(jnp.float32)
                    outbox[way, q, c] = part.astype(jnp.bfloat16)
                    hop(way, q, c).start()

        mine = rows_of(p, share)
        for way in (0, 1):

            @pl.when(p != ends[way])
            def _():
                hop(way, p, c).wait_recv()
                total[mine, cols] = total[mine, cols] + inbox[way, p, c].astype(jnp.float32)

    def one(k):
        q = (p + k) % np_
        return copy(shr.at[rows_of(q, share)], shr_in.at[k], one_send.at[k], one_recv.at[k], pool=q)

    def two(k):
        return copy(shr_sum, shr_peer.at[k], two_send.at[k], two_recv.at[k], tensor=(t + k) % nt)

    def step(c, carry):
        @pl.when(c < chunks)
        def _():
            cols = pl.ds(pl.multiple_of(c * wide, wide), wide)
            total[:, cols] = jnp.dot(
                full[...], weight[:, cols], preferred_element_type=jnp.float32
            )
            first_hops(c)

        @pl.when(c == 0)
        def _():
            lax.fori_loop(0, rows // BLK, shrink, 0)
            for k in range(1, np_):
                one(k).start()

        @pl.when(c == chunks - 1)
        def _():
            summed = shr[rows_of(p, share), :].astype(jnp.float32)
            for k in range(1, np_):
                one(k).wait_recv()
                summed = summed + shr_in[k].astype(jnp.float32)
            shr_sum[...] = summed.astype(jnp.bfloat16)
            for k in range(1, nt):
                two(k).start()

        @pl.when(c > 0)
        def _():
            later_hops(c - 1)

        return carry

    lax.fori_loop(0, chunks + 1, step, 0)

    halves = shr_sum[...].astype(jnp.float32)
    for k in range(1, nt):
        two(k).wait_recv()
        halves = halves + shr_peer[k].astype(jnp.float32)
    rank = np_ * up_mine.shape[1]
    ranks = halves[:, :rank]
    for k in range(1, halves.shape[1] // rank):
        ranks = ranks + halves[:, k * rank : (k + 1) * rank]
    shr_sum_rows = ranks.astype(jnp.bfloat16)
    ups[0] = up_mine[pl.ds(p * per_share, per_share)]
    for k in range(1, np_):
        q = (p + k) % np_
        copy(up_mine.at[pl.ds(q * per_share, per_share)], ups.at[k], up_send.at[k], up_recv.at[k], pool=q).wait_recv()
    for i in range(per_share):
        order = [ups[(p - z + np_) % np_, i].astype(jnp.float32) for z in range(np_)]
        up = jnp.concatenate(order, axis=0).astype(jnp.bfloat16)
        lines = shr_sum_rows[i * BLK : (i + 1) * BLK]
        expand = jnp.dot(lines, up, preferred_element_type=jnp.float32)
        at = pl.ds(pl.multiple_of(p * share + i * BLK, BLK), BLK)
        out[i * BLK : (i + 1) * BLK, :] = (total[at, :] + adapter_scale * expand).astype(jnp.bfloat16)

    for each in sends:
        each.wait_send()
    for k in range(1, np_):
        one(k).wait_send()
    for k in range(1, nt):
        two(k).wait_send()

    def drain(c, carry):
        for q in range(np_):
            for way in (0, 1):
                ahead = (q > p) if way == 0 else (q < p)

                @pl.when(ahead)
                def _():
                    hop(way, q, c).wait_send()

        return carry

    lax.fori_loop(0, chunks, drain, 0)


def make_local(nt, np_):
    def local(
        queries,
        key_value_cache,
        cache_lengths,
        block_adapter_slot,
        output_weight,
        adapter_down_weight,
        adapter_up_weight,
    ):
        attended = local_attention(queries, key_value_cache, cache_lengths)
        block, feat = attended.shape
        rows = block * nt
        share = rows // np_
        slots, _, rank = adapter_down_weight.shape
        columns = output_weight.shape[1]
        chunks = 4
        wide = columns // chunks
        lanes = slots * rank
        t = lax.axis_index("tensor")
        down = jnp.transpose(adapter_down_weight, (1, 0, 2)).reshape(feat, lanes)
        row_slots = jnp.repeat(block_adapter_slot, BLK)
        lane_slots = t * slots + jnp.arange(lanes, dtype=jnp.int32) // rank
        mask = (row_slots[:, None] == lane_slots[None, :]).astype(jnp.float32)
        up_mine = jnp.take(adapter_up_weight, block_adapter_slot, axis=0)
        per_share = share // BLK
        bf = jnp.bfloat16
        dma = pltpu.SemaphoreType.DMA
        boxes = (2, np_, chunks, share, wide)
        return pl.pallas_call(
            functools.partial(project_kernel, nt, np_, chunks),
            out_shape=jax.ShapeDtypeStruct((share, columns), bf),
            in_specs=[pl.BlockSpec(memory_space=pltpu.VMEM)] * 5,
            out_specs=pl.BlockSpec(memory_space=pltpu.VMEM),
            scratch_shapes=[
                pltpu.VMEM((rows, feat), bf),
                pltpu.VMEM((rows, columns), jnp.float32),
                pltpu.VMEM(boxes, bf),
                pltpu.VMEM(boxes, bf),
                pltpu.VMEM((np_, per_share, up_mine.shape[1], columns), bf),
                pltpu.VMEM((rows, lanes), bf),
                pltpu.VMEM((np_, share, lanes), bf),
                pltpu.VMEM((share, lanes), bf),
                pltpu.VMEM((nt, share, lanes), bf),
                dma((nt // 2,)), dma((nt // 2,)), dma((nt // 2,)), dma((nt // 2,)),
                dma((2, np_, chunks)), dma((2, np_, chunks)),
                dma((np_,)), dma((np_,)), dma((np_,)), dma((np_,)),
                dma((nt,)), dma((nt,)),
            ],
            compiler_params=pltpu.CompilerParams(
                collective_id=0, has_side_effects=True, vmem_limit_bytes=50 * 1024 * 1024
            ),
            cost_estimate=pl.CostEstimate(
                flops=2 * rows * feat * columns, bytes_accessed=2 * feat * columns, transcendentals=0
            ),
        )(attended, output_weight, down, mask, up_mine)

    return local


def solution(mesh):
    in_specs = (
        P(("groups", "tensor"), "pool"),
        P(("groups", "tensor"), None, None, "pool"),
        P(("groups", "tensor")),
        P("groups"),
        P("pool", "tensor"),
        P(("groups", "tensor"), "pool", None),
        P("groups", "pool", "tensor"),
    )
    out_specs = P(("groups", "pool"), "tensor")
    return jax.shard_map(make_local(mesh.shape["tensor"], mesh.shape["pool"]), mesh=mesh, in_specs=in_specs, out_specs=out_specs, check_vma=False)
```

```python
import functools
import math

import jax
import jax.numpy as jnp
from jax import lax
from jax.experimental import pallas as pl
from jax.experimental.pallas import tpu as pltpu
from jax.sharding import PartitionSpec as P

H = 64
KVH = 8
HD = 128
BLK = 128
GROUP = H // KVH

adapter_scale = 2.0


def attend_rows(rows, base, lengths, q_ref, kv_ref):
    positions, _, width = kv_ref.shape[1:]
    heads = q_ref.shape[1]
    local_kv = heads // GROUP
    owner = lax.broadcasted_iota(jnp.int32, (heads, HD), 0) // GROUP
    column = lax.broadcasted_iota(jnp.int32, (heads, positions * 2), 1)
    caches = [kv_ref[r].reshape(positions * 2, width) for r in range(rows)]
    all_scores = []
    for r in range(rows):
        q = q_ref[base + r]
        wide = jnp.concatenate(
            [jnp.where(owner == k, q, jnp.zeros_like(q)) for k in range(local_kv)], axis=1
        )
        all_scores.append(
            lax.dot_general(
                wide, caches[r], (((1,), (1,)), ((), ())), preferred_element_type=jnp.float32
            )
        )
    seen = jnp.concatenate(
        [(column % 2 + jnp.where(column < 2 * lengths[base + r], 0, 2)) for r in range(rows)], axis=0
    )
    visible = seen == 0
    scores = jnp.where(visible, jnp.concatenate(all_scores, axis=0) * (1.0 / math.sqrt(HD)), -1e30)
    expo = jnp.where(visible, jnp.exp(scores - jnp.max(scores, axis=1, keepdims=True)), 0.0)
    totals = jnp.sum(expo, axis=1, keepdims=True)
    weights = pltpu.roll(expo, 1, 1).astype(jnp.bfloat16)
    all_mixed = [
        jnp.dot(
            weights[r * heads : (r + 1) * heads], caches[r], preferred_element_type=jnp.float32
        )
        for r in range(rows)
    ]
    done = []
    for r in range(rows):
        mixed = all_mixed[r]
        picked = mixed[:, :HD]
        for k in range(1, local_kv):
            picked = jnp.where(owner == k, mixed[:, k * HD : (k + 1) * HD], picked)
        done.append((picked / totals[r * heads : (r + 1) * heads])[None])
    return jnp.concatenate(done, axis=0)


MESH = pl.DeviceIdType.MESH
PIECES = 4
STEP = 16


def project_kernel(
    nt, np_, chunks,
    lengths, queries, cache, weight_hbm, down, mask, up_mine, out,
    kv_buf, kv_sem, weight, weight_sem, full, total, inbox, outbox, ups, shr, shr_in, shr_sum, shr_peer,
    att_send, att_recv, core_send, core_recv, hop_send, hop_recv,
    up_send, up_recv, one_send, one_recv, two_send, two_recv,
):
    t, p = lax.axis_index("tensor"), lax.axis_index("pool")
    block = queries.shape[0]
    rows = full.shape[0]
    share = rows // np_
    wide = weight.shape[1] // chunks
    per_share = share // BLK

    def copy(src, dst, send, recv, **where):
        return pltpu.make_async_remote_copy(
            src_ref=src, dst_ref=dst, send_sem=send, recv_sem=recv,
            device_id=where, device_id_type=MESH,
        )

    def rows_of(index, size):
        return pl.ds(pl.multiple_of(index * size, size), size)

    group = kv_buf.shape[1]
    steps = block // group // PIECES
    piece = block // PIECES

    def fetch(i):
        return pltpu.make_async_copy(cache.at[pl.ds(i * group, group)], kv_buf.at[i % 2], kv_sem.at[i % 2])

    fetch(0).start()
    weight_copy = pltpu.make_async_copy(weight_hbm, weight, weight_sem)

    barrier = pltpu.get_barrier_semaphore()
    for k in range(1, nt):
        pl.semaphore_signal(barrier, 1, device_id={"tensor": (t + k) % nt}, device_id_type=MESH)
    for k in range(1, np_):
        pl.semaphore_signal(barrier, 1, device_id={"pool": (p + k) % np_}, device_id_type=MESH)
    pl.semaphore_wait(barrier, nt + np_ - 2)

    other = t + 1 - 2 * (t % 2)
    sends = []
    for k in range(1, np_):
        q = (p + k) % np_
        sends.append(
            copy(up_mine.at[pl.ds(q * per_share, per_share)], ups.at[k], up_send.at[k], up_recv.at[k], pool=q)
        )
    for each in sends:
        each.start()

    def part_of(owner, j):
        return full.at[rows_of(owner * PIECES + j, piece)]

    def across(k, j):
        at = part_of(t, j)
        return copy(at, at, att_send.at[k, j], att_recv.at[k, j], tensor=(t + 2 * k) % nt)

    def beside(k, j):
        at = part_of((t + nt - 2 * k) % nt, j)
        return copy(at, at, core_send.at[k, j], core_recv.at[k, j], tensor=other)

    def relay(j):
        for k in range(1, nt // 2):
            across(k, j).wait_recv()
            beside(k, j).start()

    def attend_piece(j, carry):
        def attend_step(n, carry):
            i = j * steps + n

            @pl.when(i + 1 < block // group)
            def _():
                fetch(i + 1).start()

            fetch(i).wait()
            rows_done = attend_rows(group, i * group, lengths, queries, kv_buf.at[i % 2])
            by_head = jnp.swapaxes(rows_done, 0, 1)
            at = rows_of(t * (block // group) + i, group)
            for h in range(by_head.shape[0]):
                full[at, h * HD : (h + 1) * HD] = by_head[h].astype(jnp.bfloat16)

            @pl.when(i == 0)
            def _():
                weight_copy.start()

            return carry

        lax.fori_loop(0, steps, attend_step, 0)
        for k in range(1, nt // 2):
            across(k, j).start()
        beside(0, j).start()

        @pl.when(j > 0)
        def _():
            relay(j - 1)

        return carry

    lax.fori_loop(0, PIECES, attend_piece, 0)
    relay(PIECES - 1)
    weight_copy.wait()
    for j in range(PIECES):
        for k in range(nt // 2):
            beside(k, j).wait_recv()

    def shrink(i, carry):
        at = pl.ds(pl.multiple_of(i * BLK, BLK), BLK)
        part = jnp.dot(full[at, :], down[...], preferred_element_type=jnp.float32)
        shr[at, :] = jnp.where(mask[at, :] > 0, part, 0.0).astype(jnp.bfloat16)
        return carry

    def hop(way, q, c):
        to = p + 1 if way == 0 else p - 1
        to = jnp.clip(to, 0, np_ - 1)
        return copy(
            outbox.at[way, q, c], inbox.at[way, q, c],
            hop_send.at[way, q, c], hop_recv.at[way, q, c], pool=to,
        )

    ends = (0, np_ - 1)

    def first_hops(c):
        cols = pl.ds(pl.multiple_of(c * wide, wide), wide)
        for k in range(np_ - 1):
            for way in (0, 1):
                q = np_ - 1 - k if way == 0 else k

                @pl.when(p == ends[way])
                def _():
                    part = total[q * share : (q + 1) * share, cols]
                    outbox[way, q, c] = part.astype(jnp.bfloat16)
                    hop(way, q, c).start()

    def later_hops(c):
        cols = pl.ds(pl.multiple_of(c * wide, wide), wide)
        for k in range(np_ - 1):
            for way in (0, 1):
                q = np_ - 1 - k if way == 0 else k
                ahead = (q > p) if way == 0 else (q < p)

                @pl.when(ahead & (p != ends[way]))
                def _():
                    hop(way, q, c).wait_recv()
                    part = total[q * share : (q + 1) * share, cols]
                    part = part + inbox[way, q, c].astype(jnp.float32)
                    outbox[way, q, c] = part.astype(jnp.bfloat16)
                    hop(way, q, c).start()

        mine = rows_of(p, share)
        for way in (0, 1):

            @pl.when(p != ends[way])
            def _():
                hop(way, p, c).wait_recv()
                total[mine, cols] = total[mine, cols] + inbox[way, p, c].astype(jnp.float32)

    def one(k):
        q = (p + k) % np_
        return copy(shr.at[rows_of(q, share)], shr_in.at[k], one_send.at[k], one_recv.at[k], pool=q)

    def two(k):
        return copy(shr_sum, shr_peer.at[k], two_send.at[k], two_recv.at[k], tensor=(t + k) % nt)

    def step(c, carry):
        @pl.when(c < chunks)
        def _():
            cols = pl.ds(pl.multiple_of(c * wide, wide), wide)
            total[:, cols] = jnp.dot(
                full[...], weight[:, cols], preferred_element_type=jnp.float32
            )
            first_hops(c)

        @pl.when(c == 0)
        def _():
            lax.fori_loop(0, rows // BLK, shrink, 0)
            for k in range(1, np_):
                one(k).start()

        @pl.when(c == chunks - 1)
        def _():
            summed = shr[rows_of(p, share), :].astype(jnp.float32)
            for k in range(1, np_):
                one(k).wait_recv()
                summed = summed + shr_in[k].astype(jnp.float32)
            shr_sum[...] = summed.astype(jnp.bfloat16)
            for k in range(1, nt):
                two(k).start()

        @pl.when(c > 0)
        def _():
            later_hops(c - 1)

        return carry

    lax.fori_loop(0, chunks + 1, step, 0)

    halves = shr_sum[...].astype(jnp.float32)
    for k in range(1, nt):
        two(k).wait_recv()
        halves = halves + shr_peer[k].astype(jnp.float32)
    rank = np_ * up_mine.shape[1]
    ranks = halves[:, :rank]
    for k in range(1, halves.shape[1] // rank):
        ranks = ranks + halves[:, k * rank : (k + 1) * rank]
    shr_sum_rows = ranks.astype(jnp.bfloat16)
    ups[0] = up_mine[pl.ds(p * per_share, per_share)]
    for k in range(1, np_):
        q = (p + k) % np_
        copy(up_mine.at[pl.ds(q * per_share, per_share)], ups.at[k], up_send.at[k], up_recv.at[k], pool=q).wait_recv()
    for i in range(per_share):
        order = [ups[(p - z + np_) % np_, i].astype(jnp.float32) for z in range(np_)]
        up = jnp.concatenate(order, axis=0).astype(jnp.bfloat16)
        lines = shr_sum_rows[i * BLK : (i + 1) * BLK]
        expand = jnp.dot(lines, up, preferred_element_type=jnp.float32)
        at = pl.ds(pl.multiple_of(p * share + i * BLK, BLK), BLK)
        out[i * BLK : (i + 1) * BLK, :] = (total[at, :] + adapter_scale * expand).astype(jnp.bfloat16)

    for each in sends:
        each.wait_send()
    for j in range(PIECES):
        for k in range(nt // 2):
            beside(k, j).wait_send()
        for k in range(1, nt // 2):
            across(k, j).wait_send()
    for k in range(1, np_):
        one(k).wait_send()
    for k in range(1, nt):
        two(k).wait_send()

    def drain(c, carry):
        for q in range(np_):
            for way in (0, 1):
                ahead = (q > p) if way == 0 else (q < p)

                @pl.when(ahead)
                def _():
                    hop(way, q, c).wait_send()

        return carry

    lax.fori_loop(0, chunks, drain, 0)


def make_local(nt, np_):
    def local(
        queries,
        key_value_cache,
        cache_lengths,
        block_adapter_slot,
        output_weight,
        adapter_down_weight,
        adapter_up_weight,
    ):
        block, feat = queries.shape
        rows = block * nt
        share = rows // np_
        slots, _, rank = adapter_down_weight.shape
        columns = output_weight.shape[1]
        chunks = max(1, min(8, columns // 256))
        wide = columns // chunks
        lanes = slots * rank
        t = lax.axis_index("tensor")
        down = jnp.transpose(adapter_down_weight, (1, 0, 2)).reshape(feat, lanes)
        row_slots = jnp.repeat(block_adapter_slot, BLK)
        lane_slots = t * slots + jnp.arange(lanes, dtype=jnp.int32) // rank
        mask = (row_slots[:, None] == lane_slots[None, :]).astype(jnp.float32)
        up_mine = jnp.take(adapter_up_weight, block_adapter_slot, axis=0)
        per_share = share // BLK
        bf = jnp.bfloat16
        dma = pltpu.SemaphoreType.DMA
        boxes = (2, np_, chunks, share, wide)
        return pl.pallas_call(
            functools.partial(project_kernel, nt, np_, chunks),
            out_shape=jax.ShapeDtypeStruct((share, columns), bf),
            in_specs=[
                pl.BlockSpec(memory_space=pltpu.SMEM),
                pl.BlockSpec(memory_space=pltpu.VMEM),
                pl.BlockSpec(memory_space=pl.ANY),
                pl.BlockSpec(memory_space=pl.ANY),
            ]
            + [pl.BlockSpec(memory_space=pltpu.VMEM)] * 3,
            out_specs=pl.BlockSpec(memory_space=pltpu.VMEM),
            scratch_shapes=[
                pltpu.VMEM((2, STEP) + key_value_cache.shape[1:], bf),
                dma((2,)),
                pltpu.VMEM((feat, columns), bf),
                dma,
                pltpu.VMEM((rows, feat), bf),
                pltpu.VMEM((rows, columns), jnp.float32),
                pltpu.VMEM(boxes, bf),
                pltpu.VMEM(boxes, bf),
                pltpu.VMEM((np_, per_share, up_mine.shape[1], columns), bf),
                pltpu.VMEM((rows, lanes), bf),
                pltpu.VMEM((np_, share, lanes), bf),
                pltpu.VMEM((share, lanes), bf),
                pltpu.VMEM((nt, share, lanes), bf),
                dma((nt // 2, PIECES)), dma((nt // 2, PIECES)), dma((nt // 2, PIECES)), dma((nt // 2, PIECES)),
                dma((2, np_, chunks)), dma((2, np_, chunks)),
                dma((np_,)), dma((np_,)), dma((np_,)), dma((np_,)),
                dma((nt,)), dma((nt,)),
            ],
            compiler_params=pltpu.CompilerParams(
                collective_id=0, has_side_effects=True, vmem_limit_bytes=50 * 1024 * 1024
            ),
            cost_estimate=pl.CostEstimate(
                flops=2 * rows * feat * columns, bytes_accessed=2 * feat * columns, transcendentals=0
            ),
        )(
            cache_lengths, queries.reshape(block, feat // HD, HD), key_value_cache, output_weight,
            down, mask, up_mine,
        )

    return local


def solution(mesh):
    in_specs = (
        P(("groups", "tensor"), "pool"),
        P(("groups", "tensor"), None, None, "pool"),
        P(("groups", "tensor")),
        P("groups"),
        P("pool", "tensor"),
        P(("groups", "tensor"), "pool", None),
        P("groups", "pool", "tensor"),
    )
    out_specs = P(("groups", "pool"), "tensor")
    return jax.shard_map(make_local(mesh.shape["tensor"], mesh.shape["pool"]), mesh=mesh, in_specs=in_specs, out_specs=out_specs, check_vma=False)
```

```python
import functools
import math

import jax
import jax.numpy as jnp
from jax import lax
from jax.experimental import pallas as pl
from jax.experimental.pallas import tpu as pltpu
from jax.sharding import PartitionSpec as P

H = 64
KVH = 8
HD = 128
BLK = 128
GROUP = H // KVH

adapter_scale = 2.0


def attend_rows(rows, base, lengths, q_ref, kv_ref):
    positions, _, width = kv_ref.shape[1:]
    heads = q_ref.shape[1]
    local_kv = heads // GROUP
    owner = lax.broadcasted_iota(jnp.int32, (heads, HD), 0) // GROUP
    column = lax.broadcasted_iota(jnp.int32, (heads, positions * 2), 1)
    caches = [kv_ref[r].reshape(positions * 2, width) for r in range(rows)]
    all_scores = []
    for r in range(rows):
        q = q_ref[base + r]
        wide = jnp.concatenate(
            [jnp.where(owner == k, q, jnp.zeros_like(q)) for k in range(local_kv)], axis=1
        )
        all_scores.append(
            lax.dot_general(
                wide, caches[r], (((1,), (1,)), ((), ())), preferred_element_type=jnp.float32
            )
        )
    seen = jnp.concatenate(
        [(column % 2 + jnp.where(column < 2 * lengths[base + r], 0, 2)) for r in range(rows)], axis=0
    )
    visible = seen == 0
    scores = jnp.where(visible, jnp.concatenate(all_scores, axis=0) * (1.0 / math.sqrt(HD)), -1e30)
    expo = jnp.where(visible, jnp.exp(scores - jnp.max(scores, axis=1, keepdims=True)), 0.0)
    totals = jnp.sum(expo, axis=1, keepdims=True)
    weights = pltpu.roll(expo, 1, 1).astype(jnp.bfloat16)
    all_mixed = [
        jnp.dot(
            weights[r * heads : (r + 1) * heads], caches[r], preferred_element_type=jnp.float32
        )
        for r in range(rows)
    ]
    done = []
    for r in range(rows):
        mixed = all_mixed[r]
        picked = mixed[:, :HD]
        for k in range(1, local_kv):
            picked = jnp.where(owner == k, mixed[:, k * HD : (k + 1) * HD], picked)
        done.append((picked / totals[r * heads : (r + 1) * heads])[None])
    return jnp.concatenate(done, axis=0)


MESH = pl.DeviceIdType.MESH
PIECES = 4
STEP = 16


def project_kernel(
    nt, np_, chunks,
    lengths, queries, cache, weight_hbm, down, mask, up_mine, out,
    kv_buf, kv_sem, weight, weight_sem, full, total, inbox, outbox, ups, shr, shr_in, shr_sum, shr_peer,
    att_send, att_recv, core_send, core_recv, hop_send, hop_recv,
    up_send, up_recv, one_send, one_recv, two_send, two_recv,
):
    t, p = lax.axis_index("tensor"), lax.axis_index("pool")
    block = queries.shape[0]
    rows = full.shape[0]
    share = rows // np_
    wide = weight.shape[1] // chunks
    per_share = share // BLK

    def copy(src, dst, send, recv, **where):
        return pltpu.make_async_remote_copy(
            src_ref=src, dst_ref=dst, send_sem=send, recv_sem=recv,
            device_id=where, device_id_type=MESH,
        )

    def rows_of(index, size):
        return pl.ds(pl.multiple_of(index * size, size), size)

    group = kv_buf.shape[1]
    steps = block // group // PIECES
    piece = block // PIECES

    def fetch(i):
        return pltpu.make_async_copy(cache.at[pl.ds(i * group, group)], kv_buf.at[i % 2], kv_sem.at[i % 2])

    fetch(0).start()
    weight_copy = pltpu.make_async_copy(weight_hbm, weight, weight_sem)

    barrier = pltpu.get_barrier_semaphore()
    for k in range(1, nt):
        pl.semaphore_signal(barrier, 1, device_id={"tensor": (t + k) % nt}, device_id_type=MESH)
    for k in range(1, np_):
        pl.semaphore_signal(barrier, 1, device_id={"pool": (p + k) % np_}, device_id_type=MESH)
    pl.semaphore_wait(barrier, nt + np_ - 2)

    other = t + 1 - 2 * (t % 2)
    sends = []
    for k in range(1, np_):
        q = (p + k) % np_
        sends.append(
            copy(up_mine.at[pl.ds(q * per_share, per_share)], ups.at[k], up_send.at[k], up_recv.at[k], pool=q)
        )
    for each in sends:
        each.start()

    def part_of(owner, j):
        return full.at[rows_of(owner * PIECES + j, piece)]

    def across(k, j):
        at = part_of(t, j)
        return copy(at, at, att_send.at[k, j], att_recv.at[k, j], tensor=(t + 2 * k) % nt)

    def beside(k, j):
        at = part_of((t + nt - 2 * k) % nt, j)
        return copy(at, at, core_send.at[k, j], core_recv.at[k, j], tensor=other)

    def relay(j):
        for k in range(1, nt // 2):
            across(k, j).wait_recv()
            beside(k, j).start()

    def attend_piece(j, carry):
        def attend_step(n, carry):
            i = j * steps + n

            @pl.when(i + 1 < block // group)
            def _():
                fetch(i + 1).start()

            fetch(i).wait()
            rows_done = attend_rows(group, i * group, lengths, queries, kv_buf.at[i % 2])
            by_head = jnp.swapaxes(rows_done, 0, 1)
            at = rows_of(t * (block // group) + i, group)
            for h in range(by_head.shape[0]):
                full[at, h * HD : (h + 1) * HD] = by_head[h].astype(jnp.bfloat16)

            @pl.when(i == 0)
            def _():
                weight_copy.start()

            return carry

        lax.fori_loop(0, steps, attend_step, 0)
        for k in range(1, nt // 2):
            across(k, j).start()
        beside(0, j).start()

        @pl.when(j > 0)
        def _():
            relay(j - 1)

        return carry

    lax.fori_loop(0, PIECES, attend_piece, 0)
    relay(PIECES - 1)
    weight_copy.wait()
    for j in range(PIECES):
        for k in range(nt // 2):
            beside(k, j).wait_recv()

    def shrink(i, carry):
        at = pl.ds(pl.multiple_of(i * BLK, BLK), BLK)
        part = jnp.dot(full[at, :], down[...], preferred_element_type=jnp.float32)
        shr[at, :] = jnp.where(mask[at, :] > 0, part, 0.0).astype(jnp.bfloat16)
        return carry

    def hop(way, q, c):
        to = p + 1 if way == 0 else p - 1
        to = jnp.clip(to, 0, np_ - 1)
        return copy(
            outbox.at[way, q, c], inbox.at[way, q, c],
            hop_send.at[way, q, c], hop_recv.at[way, q, c], pool=to,
        )

    ends = (0, np_ - 1)

    def hops(c):
        behind = (p, np_ - 1 - p)
        for k in range(np_):
            for way in (0, 1):
                q = np_ - 1 - k if way == 0 else k
                ahead = (q > p) if way == 0 else (q < p)
                at = c - behind[way]
                inside = (at >= 0) & (at < chunks)
                d = jnp.clip(at, 0, chunks - 1)
                cols = pl.ds(pl.multiple_of(d * wide, wide), wide)
                lines = slice(q * share, (q + 1) * share)

                @pl.when(inside & ahead & (behind[way] == 0))
                def _():
                    outbox[way, q, d] = total[lines, cols].astype(jnp.bfloat16)
                    hop(way, q, d).start()

                @pl.when(inside & ahead & (behind[way] > 0))
                def _():
                    hop(way, q, d).wait_recv()
                    part = total[lines, cols] + inbox[way, q, d].astype(jnp.float32)
                    outbox[way, q, d] = part.astype(jnp.bfloat16)
                    hop(way, q, d).start()

                @pl.when(inside & (p == q) & (behind[way] > 0))
                def _():
                    hop(way, q, d).wait_recv()
                    total[lines, cols] = total[lines, cols] + inbox[way, q, d].astype(jnp.float32)

    def one(k):
        q = (p + k) % np_
        return copy(shr.at[rows_of(q, share)], shr_in.at[k], one_send.at[k], one_recv.at[k], pool=q)

    def two(k):
        return copy(shr_sum, shr_peer.at[k], two_send.at[k], two_recv.at[k], tensor=(t + k) % nt)

    def step(c, carry):
        @pl.when(c < chunks)
        def _():
            cols = pl.ds(pl.multiple_of(c * wide, wide), wide)
            total[:, cols] = jnp.dot(
                full[...], weight[:, cols], preferred_element_type=jnp.float32
            )

        hops(c)

        @pl.when(c == 0)
        def _():
            lax.fori_loop(0, rows // BLK, shrink, 0)
            for k in range(1, np_):
                one(k).start()

        @pl.when(c == chunks - 1)
        def _():
            summed = shr[rows_of(p, share), :].astype(jnp.float32)
            for k in range(1, np_):
                one(k).wait_recv()
                summed = summed + shr_in[k].astype(jnp.float32)
            shr_sum[...] = summed.astype(jnp.bfloat16)
            for k in range(1, nt):
                two(k).start()

        return carry

    lax.fori_loop(0, chunks + np_ - 1, step, 0)

    halves = shr_sum[...].astype(jnp.float32)
    for k in range(1, nt):
        two(k).wait_recv()
        halves = halves + shr_peer[k].astype(jnp.float32)
    rank = np_ * up_mine.shape[1]
    ranks = halves[:, :rank]
    for k in range(1, halves.shape[1] // rank):
        ranks = ranks + halves[:, k * rank : (k + 1) * rank]
    shr_sum_rows = ranks.astype(jnp.bfloat16)
    ups[0] = up_mine[pl.ds(p * per_share, per_share)]
    for k in range(1, np_):
        q = (p + k) % np_
        copy(up_mine.at[pl.ds(q * per_share, per_share)], ups.at[k], up_send.at[k], up_recv.at[k], pool=q).wait_recv()
    for i in range(per_share):
        order = [ups[(p - z + np_) % np_, i].astype(jnp.float32) for z in range(np_)]
        up = jnp.concatenate(order, axis=0).astype(jnp.bfloat16)
        lines = shr_sum_rows[i * BLK : (i + 1) * BLK]
        expand = jnp.dot(lines, up, preferred_element_type=jnp.float32)
        at = pl.ds(pl.multiple_of(p * share + i * BLK, BLK), BLK)
        out[i * BLK : (i + 1) * BLK, :] = (total[at, :] + adapter_scale * expand).astype(jnp.bfloat16)

    for each in sends:
        each.wait_send()
    for j in range(PIECES):
        for k in range(nt // 2):
            beside(k, j).wait_send()
        for k in range(1, nt // 2):
            across(k, j).wait_send()
    for k in range(1, np_):
        one(k).wait_send()
    for k in range(1, nt):
        two(k).wait_send()

    def drain(c, carry):
        for q in range(np_):
            for way in (0, 1):
                ahead = (q > p) if way == 0 else (q < p)

                @pl.when(ahead)
                def _():
                    hop(way, q, c).wait_send()

        return carry

    lax.fori_loop(0, chunks, drain, 0)


def make_local(nt, np_):
    def local(
        queries,
        key_value_cache,
        cache_lengths,
        block_adapter_slot,
        output_weight,
        adapter_down_weight,
        adapter_up_weight,
    ):
        block, feat = queries.shape
        rows = block * nt
        share = rows // np_
        slots, _, rank = adapter_down_weight.shape
        columns = output_weight.shape[1]
        chunks = max(1, min(8, columns // 256))
        wide = columns // chunks
        lanes = slots * rank
        t = lax.axis_index("tensor")
        down = jnp.transpose(adapter_down_weight, (1, 0, 2)).reshape(feat, lanes)
        row_slots = jnp.repeat(block_adapter_slot, BLK)
        lane_slots = t * slots + jnp.arange(lanes, dtype=jnp.int32) // rank
        mask = (row_slots[:, None] == lane_slots[None, :]).astype(jnp.float32)
        up_mine = jnp.take(adapter_up_weight, block_adapter_slot, axis=0)
        per_share = share // BLK
        bf = jnp.bfloat16
        dma = pltpu.SemaphoreType.DMA
        boxes = (2, np_, chunks, share, wide)
        return pl.pallas_call(
            functools.partial(project_kernel, nt, np_, chunks),
            out_shape=jax.ShapeDtypeStruct((share, columns), bf),
            in_specs=[
                pl.BlockSpec(memory_space=pltpu.SMEM),
                pl.BlockSpec(memory_space=pltpu.VMEM),
                pl.BlockSpec(memory_space=pl.ANY),
                pl.BlockSpec(memory_space=pl.ANY),
            ]
            + [pl.BlockSpec(memory_space=pltpu.VMEM)] * 3,
            out_specs=pl.BlockSpec(memory_space=pltpu.VMEM),
            scratch_shapes=[
                pltpu.VMEM((2, STEP) + key_value_cache.shape[1:], bf),
                dma((2,)),
                pltpu.VMEM((feat, columns), bf),
                dma,
                pltpu.VMEM((rows, feat), bf),
                pltpu.VMEM((rows, columns), jnp.float32),
                pltpu.VMEM(boxes, bf),
                pltpu.VMEM(boxes, bf),
                pltpu.VMEM((np_, per_share, up_mine.shape[1], columns), bf),
                pltpu.VMEM((rows, lanes), bf),
                pltpu.VMEM((np_, share, lanes), bf),
                pltpu.VMEM((share, lanes), bf),
                pltpu.VMEM((nt, share, lanes), bf),
                dma((nt // 2, PIECES)), dma((nt // 2, PIECES)), dma((nt // 2, PIECES)), dma((nt // 2, PIECES)),
                dma((2, np_, chunks)), dma((2, np_, chunks)),
                dma((np_,)), dma((np_,)), dma((np_,)), dma((np_,)),
                dma((nt,)), dma((nt,)),
            ],
            compiler_params=pltpu.CompilerParams(
                collective_id=0, has_side_effects=True, vmem_limit_bytes=50 * 1024 * 1024
            ),
            cost_estimate=pl.CostEstimate(
                flops=2 * rows * feat * columns, bytes_accessed=2 * feat * columns, transcendentals=0
            ),
        )(
            cache_lengths, queries.reshape(block, feat // HD, HD), key_value_cache, output_weight,
            down, mask, up_mine,
        )

    return local


def solution(mesh):
    in_specs = (
        P(("groups", "tensor"), "pool"),
        P(("groups", "tensor"), None, None, "pool"),
        P(("groups", "tensor")),
        P("groups"),
        P("pool", "tensor"),
        P(("groups", "tensor"), "pool", None),
        P("groups", "pool", "tensor"),
    )
    out_specs = P(("groups", "pool"), "tensor")
    return jax.shard_map(make_local(mesh.shape["tensor"], mesh.shape["pool"]), mesh=mesh, in_specs=in_specs, out_specs=out_specs, check_vma=False)
```

```python
import functools
import math

import jax
import jax.numpy as jnp
from jax import lax
from jax.experimental import pallas as pl
from jax.experimental.pallas import tpu as pltpu
from jax.sharding import PartitionSpec as P

H = 64
KVH = 8
HD = 128
BLK = 128
GROUP = H // KVH

adapter_scale = 2.0


def attend_rows(rows, base, lengths, q_ref, kv_ref):
    positions, _, width = kv_ref.shape[1:]
    heads = q_ref.shape[1]
    local_kv = heads // GROUP
    owner = lax.broadcasted_iota(jnp.int32, (heads, HD), 0) // GROUP
    column = lax.broadcasted_iota(jnp.int32, (heads, positions * 2), 1)
    caches = [kv_ref[r].reshape(positions * 2, width) for r in range(rows)]
    all_scores = []
    for r in range(rows):
        q = q_ref[base + r]
        wide = jnp.concatenate(
            [jnp.where(owner == k, q, jnp.zeros_like(q)) for k in range(local_kv)], axis=1
        )
        all_scores.append(
            lax.dot_general(
                wide, caches[r], (((1,), (1,)), ((), ())), preferred_element_type=jnp.float32
            )
        )
    seen = jnp.concatenate(
        [(column % 2 + jnp.where(column < 2 * lengths[base + r], 0, 2)) for r in range(rows)], axis=0
    )
    visible = seen == 0
    scores = jnp.where(visible, jnp.concatenate(all_scores, axis=0) * (1.0 / math.sqrt(HD)), -1e30)
    expo = jnp.where(visible, jnp.exp(scores - jnp.max(scores, axis=1, keepdims=True)), 0.0)
    totals = jnp.sum(expo, axis=1, keepdims=True)
    weights = pltpu.roll(expo, 1, 1).astype(jnp.bfloat16)
    all_mixed = [
        jnp.dot(
            weights[r * heads : (r + 1) * heads], caches[r], preferred_element_type=jnp.float32
        )
        for r in range(rows)
    ]
    done = []
    for r in range(rows):
        mixed = all_mixed[r]
        picked = mixed[:, :HD]
        for k in range(1, local_kv):
            picked = jnp.where(owner == k, mixed[:, k * HD : (k + 1) * HD], picked)
        done.append((picked / totals[r * heads : (r + 1) * heads])[None])
    return jnp.concatenate(done, axis=0)


MESH = pl.DeviceIdType.MESH
PIECES = 2
STEP = 16


def project_kernel(
    nt, np_, chunks,
    lengths, queries, cache, weight_hbm, down, mask, up_mine, out,
    kv_buf, kv_sem, weight, weight_sem, full, total, inbox, outbox, ups, shr, shr_in, shr_sum, shr_peer,
    att_send, att_recv, core_send, core_recv, hop_send, hop_recv,
    up_send, up_recv, one_send, one_recv, two_send, two_recv,
):
    t, p = lax.axis_index("tensor"), lax.axis_index("pool")
    block = queries.shape[0]
    rows = full.shape[0]
    share = rows // np_
    wide = weight.shape[1] // chunks
    per_share = share // BLK
    half = rows // PIECES
    part_share = share // PIECES

    def copy(src, dst, send, recv, **where):
        return pltpu.make_async_remote_copy(
            src_ref=src, dst_ref=dst, send_sem=send, recv_sem=recv,
            device_id=where, device_id_type=MESH,
        )

    def rows_of(index, size):
        return pl.ds(pl.multiple_of(index * size, size), size)

    group = kv_buf.shape[1]
    steps = block // group // PIECES
    piece = block // PIECES

    def fetch(i):
        return pltpu.make_async_copy(cache.at[pl.ds(i * group, group)], kv_buf.at[i % 2], kv_sem.at[i % 2])

    fetch(0).start()
    weight_copy = pltpu.make_async_copy(weight_hbm, weight, weight_sem)

    barrier = pltpu.get_barrier_semaphore()
    for k in range(1, nt):
        pl.semaphore_signal(barrier, 1, device_id={"tensor": (t + k) % nt}, device_id_type=MESH)
    for k in range(1, np_):
        pl.semaphore_signal(barrier, 1, device_id={"pool": (p + k) % np_}, device_id_type=MESH)
    pl.semaphore_wait(barrier, nt + np_ - 2)

    other = t + 1 - 2 * (t % 2)
    sends = []
    for k in range(1, np_):
        q = (p + k) % np_
        sends.append(
            copy(up_mine.at[pl.ds(q * per_share, per_share)], ups.at[k], up_send.at[k], up_recv.at[k], pool=q)
        )
    for each in sends:
        each.start()

    def part_of(owner, j):
        return full.at[rows_of(j * nt + owner, piece)]

    def across(k, j):
        at = part_of(t, j)
        return copy(at, at, att_send.at[k, j], att_recv.at[k, j], tensor=(t + 2 * k) % nt)

    def beside(k, j):
        at = part_of((t + nt - 2 * k) % nt, j)
        return copy(at, at, core_send.at[k, j], core_recv.at[k, j], tensor=other)

    def relay(j):
        for k in range(1, nt // 2):
            across(k, j).wait_recv()
            beside(k, j).start()

    def attend_step(i, carry):
        @pl.when(i + 1 < block // group)
        def _():
            fetch(i + 1).start()

        fetch(i).wait()
        rows_done = attend_rows(group, i * group, lengths, queries, kv_buf.at[i % 2])
        by_head = jnp.swapaxes(rows_done, 0, 1)
        at = rows_of(((i // steps) * nt + t) * steps + i % steps, group)
        for h in range(by_head.shape[0]):
            full[at, h * HD : (h + 1) * HD] = by_head[h].astype(jnp.bfloat16)

        @pl.when(i == 0)
        def _():
            weight_copy.start()

        return carry

    def send_piece(j):
        for k in range(1, nt // 2):
            across(k, j).start()
        beside(0, j).start()

    def wait_piece(j):
        for k in range(nt // 2):
            beside(k, j).wait_recv()

    lax.fori_loop(0, steps, attend_step, 0)
    send_piece(0)
    relay(0)
    weight_copy.wait()
    wait_piece(0)

    def shrink(j):
        at = slice(j * half, (j + 1) * half)
        part = jnp.dot(full[at, :], down[...], preferred_element_type=jnp.float32)
        part = jnp.where(mask[at, :] > 0, part, 0.0).astype(jnp.bfloat16)
        for q in range(np_):
            shr[q, j * part_share : (j + 1) * part_share, :] = part[q * part_share : (q + 1) * part_share]

    def hop(way, q, c):
        to = p + 1 if way == 0 else p - 1
        to = jnp.clip(to, 0, np_ - 1)
        return copy(
            outbox.at[way, q, c], inbox.at[way, q, c],
            hop_send.at[way, q, c], hop_recv.at[way, q, c], pool=to,
        )

    turns = PIECES * chunks
    busy = min(2, chunks)

    def hops(c):
        behind = (p, np_ - 1 - p)
        for k in range(np_):
            for way in (0, 1):
                q = np_ - 1 - k if way == 0 else k
                ahead = (q > p) if way == 0 else (q < p)
                at = c - behind[way]
                inside = (at >= 0) & (at < turns)
                d = jnp.clip(at, 0, turns - 1)
                cols = pl.ds(pl.multiple_of(d % chunks * wide, wide), wide)
                lines = rows_of(d // chunks * np_ + q, part_share)

                @pl.when(inside & ahead & (behind[way] == 0))
                def _():
                    outbox[way, q, d] = total[lines, cols].astype(jnp.bfloat16)
                    hop(way, q, d).start()

                @pl.when(inside & ahead & (behind[way] > 0))
                def _():
                    hop(way, q, d).wait_recv()
                    part = total[lines, cols] + inbox[way, q, d].astype(jnp.float32)
                    outbox[way, q, d] = part.astype(jnp.bfloat16)
                    hop(way, q, d).start()

                @pl.when(inside & (p == q) & (behind[way] > 0))
                def _():
                    hop(way, q, d).wait_recv()
                    total[lines, cols] = total[lines, cols] + inbox[way, q, d].astype(jnp.float32)

    def one(k):
        q = (p + k) % np_
        return copy(shr.at[q], shr_in.at[k], one_send.at[k], one_recv.at[k], pool=q)

    def two(k):
        return copy(shr_sum, shr_peer.at[k], two_send.at[k], two_recv.at[k], tensor=(t + k) % nt)

    def step(c, carry):
        @pl.when(c == chunks)
        def _():
            wait_piece(1)

        @pl.when(c < turns)
        def _():
            cols = pl.ds(pl.multiple_of(c % chunks * wide, wide), wide)
            lines = rows_of(c // chunks, half)
            total[lines, cols] = jnp.dot(
                full[lines, :], weight[:, cols], preferred_element_type=jnp.float32
            )

        hops(c)

        @pl.when(c < busy)
        def _():
            each = steps // busy
            lax.fori_loop(steps + c * each, steps + (c + 1) * each, attend_step, 0)

        @pl.when(c == busy - 1)
        def _():
            send_piece(1)

        @pl.when(c == chunks - 1)
        def _():
            shrink(0)
            relay(1)

        @pl.when(c == chunks)
        def _():
            shrink(1)
            for k in range(1, np_):
                one(k).start()

        @pl.when(c == turns)
        def _():
            summed = shr[p].astype(jnp.float32)
            for k in range(1, np_):
                one(k).wait_recv()
                summed = summed + shr_in[k].astype(jnp.float32)
            shr_sum[...] = summed.astype(jnp.bfloat16)
            for k in range(1, nt):
                two(k).start()

        return carry

    lax.fori_loop(0, turns + np_ - 1, step, 0)

    halves = shr_sum[...].astype(jnp.float32)
    for k in range(1, nt):
        two(k).wait_recv()
        halves = halves + shr_peer[k].astype(jnp.float32)
    rank = np_ * up_mine.shape[1]
    ranks = halves[:, :rank]
    for k in range(1, halves.shape[1] // rank):
        ranks = ranks + halves[:, k * rank : (k + 1) * rank]
    shr_sum_rows = ranks.astype(jnp.bfloat16)
    ups[0] = up_mine[pl.ds(p * per_share, per_share)]
    for k in range(1, np_):
        q = (p + k) % np_
        copy(up_mine.at[pl.ds(q * per_share, per_share)], ups.at[k], up_send.at[k], up_recv.at[k], pool=q).wait_recv()
    for i in range(per_share):
        order = [ups[(p - z + np_) % np_, i].astype(jnp.float32) for z in range(np_)]
        up = jnp.concatenate(order, axis=0).astype(jnp.bfloat16)
        for j in range(PIECES):
            first = j * part_share + i * piece
            expand = jnp.dot(
                shr_sum_rows[first : first + piece], up, preferred_element_type=jnp.float32
            )
            at = rows_of(j * (half // piece) + p * per_share + i, piece)
            to = i * BLK + j * piece
            out[to : to + piece, :] = (total[at, :] + adapter_scale * expand).astype(jnp.bfloat16)

    for each in sends:
        each.wait_send()
    for j in range(PIECES):
        for k in range(nt // 2):
            beside(k, j).wait_send()
        for k in range(1, nt // 2):
            across(k, j).wait_send()
    for k in range(1, np_):
        one(k).wait_send()
    for k in range(1, nt):
        two(k).wait_send()

    def drain(c, carry):
        for q in range(np_):
            for way in (0, 1):
                ahead = (q > p) if way == 0 else (q < p)

                @pl.when(ahead)
                def _():
                    hop(way, q, c).wait_send()

        return carry

    lax.fori_loop(0, turns, drain, 0)


def make_local(nt, np_):
    def local(
        queries,
        key_value_cache,
        cache_lengths,
        block_adapter_slot,
        output_weight,
        adapter_down_weight,
        adapter_up_weight,
    ):
        block, feat = queries.shape
        rows = block * nt
        share = rows // np_
        slots, _, rank = adapter_down_weight.shape
        columns = output_weight.shape[1]
        chunks = max(1, min(4, columns // 512))
        wide = columns // chunks
        lanes = slots * rank
        t = lax.axis_index("tensor")
        down = jnp.transpose(adapter_down_weight, (1, 0, 2)).reshape(feat, lanes)
        row_slots = jnp.tile(jnp.repeat(block_adapter_slot, BLK // PIECES), PIECES)
        lane_slots = t * slots + jnp.arange(lanes, dtype=jnp.int32) // rank
        mask = (row_slots[:, None] == lane_slots[None, :]).astype(jnp.float32)
        up_mine = jnp.take(adapter_up_weight, block_adapter_slot, axis=0)
        per_share = share // BLK
        bf = jnp.bfloat16
        dma = pltpu.SemaphoreType.DMA
        boxes = (2, np_, PIECES * chunks, share // PIECES, wide)
        return pl.pallas_call(
            functools.partial(project_kernel, nt, np_, chunks),
            out_shape=jax.ShapeDtypeStruct((share, columns), bf),
            in_specs=[
                pl.BlockSpec(memory_space=pltpu.SMEM),
                pl.BlockSpec(memory_space=pltpu.VMEM),
                pl.BlockSpec(memory_space=pl.ANY),
                pl.BlockSpec(memory_space=pl.ANY),
            ]
            + [pl.BlockSpec(memory_space=pltpu.VMEM)] * 3,
            out_specs=pl.BlockSpec(memory_space=pltpu.VMEM),
            scratch_shapes=[
                pltpu.VMEM((2, STEP) + key_value_cache.shape[1:], bf),
                dma((2,)),
                pltpu.VMEM((feat, columns), bf),
                dma,
                pltpu.VMEM((rows, feat), bf),
                pltpu.VMEM((rows, columns), jnp.float32),
                pltpu.VMEM(boxes, bf),
                pltpu.VMEM(boxes, bf),
                pltpu.VMEM((np_, per_share, up_mine.shape[1], columns), bf),
                pltpu.VMEM((np_, share, lanes), bf),
                pltpu.VMEM((np_, share, lanes), bf),
                pltpu.VMEM((share, lanes), bf),
                pltpu.VMEM((nt, share, lanes), bf),
                dma((nt // 2, PIECES)), dma((nt // 2, PIECES)), dma((nt // 2, PIECES)), dma((nt // 2, PIECES)),
                dma((2, np_, PIECES * chunks)), dma((2, np_, PIECES * chunks)),
                dma((np_,)), dma((np_,)), dma((np_,)), dma((np_,)),
                dma((nt,)), dma((nt,)),
            ],
            compiler_params=pltpu.CompilerParams(
                collective_id=0, has_side_effects=True, vmem_limit_bytes=50 * 1024 * 1024
            ),
            cost_estimate=pl.CostEstimate(
                flops=2 * rows * feat * columns, bytes_accessed=2 * feat * columns, transcendentals=0
            ),
        )(
            cache_lengths, queries.reshape(block, feat // HD, HD), key_value_cache, output_weight,
            down, mask, up_mine,
        )

    return local


def solution(mesh):
    in_specs = (
        P(("groups", "tensor"), "pool"),
        P(("groups", "tensor"), None, None, "pool"),
        P(("groups", "tensor")),
        P("groups"),
        P("pool", "tensor"),
        P(("groups", "tensor"), "pool", None),
        P("groups", "pool", "tensor"),
    )
    out_specs = P(("groups", "pool"), "tensor")
    return jax.shard_map(make_local(mesh.shape["tensor"], mesh.shape["pool"]), mesh=mesh, in_specs=in_specs, out_specs=out_specs, check_vma=False)
```

```python
import functools
import math

import jax
import jax.numpy as jnp
from jax import lax
from jax.experimental import pallas as pl
from jax.experimental.pallas import tpu as pltpu
from jax.sharding import PartitionSpec as P

H = 64
KVH = 8
HD = 128
BLK = 128
GROUP = H // KVH

adapter_scale = 2.0


def attend_rows(rows, base, lengths, q_ref, kv_ref):
    positions, _, width = kv_ref.shape[1:]
    heads = q_ref.shape[1]
    local_kv = heads // GROUP
    owner = lax.broadcasted_iota(jnp.int32, (heads, HD), 0) // GROUP
    column = lax.broadcasted_iota(jnp.int32, (heads, positions * 2), 1)
    caches = [kv_ref[r].reshape(positions * 2, width) for r in range(rows)]
    all_scores = []
    for r in range(rows):
        q = q_ref[base + r]
        wide = jnp.concatenate(
            [jnp.where(owner == k, q, jnp.zeros_like(q)) for k in range(local_kv)], axis=1
        )
        all_scores.append(
            lax.dot_general(
                wide, caches[r], (((1,), (1,)), ((), ())), preferred_element_type=jnp.float32
            )
        )
    seen = jnp.concatenate(
        [(column % 2 + jnp.where(column < 2 * lengths[base + r], 0, 2)) for r in range(rows)], axis=0
    )
    visible = seen == 0
    scores = jnp.where(visible, jnp.concatenate(all_scores, axis=0) * (1.0 / math.sqrt(HD)), -1e30)
    expo = jnp.where(visible, jnp.exp(scores - jnp.max(scores, axis=1, keepdims=True)), 0.0)
    totals = jnp.sum(expo, axis=1, keepdims=True)
    weights = pltpu.roll(expo, 1, 1).astype(jnp.bfloat16)
    all_mixed = [
        jnp.dot(
            weights[r * heads : (r + 1) * heads], caches[r], preferred_element_type=jnp.float32
        )
        for r in range(rows)
    ]
    done = []
    for r in range(rows):
        mixed = all_mixed[r]
        picked = mixed[:, :HD]
        for k in range(1, local_kv):
            picked = jnp.where(owner == k, mixed[:, k * HD : (k + 1) * HD], picked)
        done.append((picked / totals[r * heads : (r + 1) * heads])[None])
    return jnp.concatenate(done, axis=0)


MESH = pl.DeviceIdType.MESH
PIECES = 2
STEP = 16


def project_kernel(
    nt, np_, chunks,
    lengths, queries, cache, weight_hbm, down, slots, up_all, out,
    up_mine, kv_buf, kv_sem, weight, weight_sem, full, total, inbox, outbox, ups, shr, shr_in, shr_sum, shr_peer,
    att_send, att_recv, core_send, core_recv, hop_send, hop_recv,
    up_send, up_recv, one_send, one_recv, two_send, two_recv,
):
    t, p = lax.axis_index("tensor"), lax.axis_index("pool")
    block = queries.shape[0]
    rows = full.shape[0]
    share = rows // np_
    wide = weight.shape[1] // chunks
    per_share = share // BLK
    half = rows // PIECES
    part_share = share // PIECES

    def copy(src, dst, send, recv, **where):
        return pltpu.make_async_remote_copy(
            src_ref=src, dst_ref=dst, send_sem=send, recv_sem=recv,
            device_id=where, device_id_type=MESH,
        )

    def rows_of(index, size):
        return pl.ds(pl.multiple_of(index * size, size), size)

    group = kv_buf.shape[1]
    steps = block // group // PIECES
    piece = block // PIECES

    def fetch(i):
        return pltpu.make_async_copy(cache.at[pl.ds(i * group, group)], kv_buf.at[i % 2], kv_sem.at[i % 2])

    fetch(0).start()
    weight_copy = pltpu.make_async_copy(weight_hbm, weight, weight_sem)

    barrier = pltpu.get_barrier_semaphore()
    for k in range(1, nt):
        pl.semaphore_signal(barrier, 1, device_id={"tensor": (t + k) % nt}, device_id_type=MESH)
    for k in range(1, np_):
        pl.semaphore_signal(barrier, 1, device_id={"pool": (p + k) % np_}, device_id_type=MESH)
    pl.semaphore_wait(barrier, nt + np_ - 2)

    other = t + 1 - 2 * (t % 2)
    for b in range(rows // BLK):
        up_mine[b] = up_all[slots[b]]
    sends = []
    for k in range(1, np_):
        q = (p + k) % np_
        sends.append(
            copy(up_mine.at[pl.ds(q * per_share, per_share)], ups.at[k], up_send.at[k], up_recv.at[k], pool=q)
        )
    for each in sends:
        each.start()

    def part_of(owner, j):
        return full.at[rows_of(j * nt + owner, piece)]

    def across(k, j):
        at = part_of(t, j)
        return copy(at, at, att_send.at[k, j], att_recv.at[k, j], tensor=(t + 2 * k) % nt)

    def beside(k, j):
        at = part_of((t + nt - 2 * k) % nt, j)
        return copy(at, at, core_send.at[k, j], core_recv.at[k, j], tensor=other)

    def relay(j):
        for k in range(1, nt // 2):
            across(k, j).wait_recv()
            beside(k, j).start()

    def attend_step(i, carry):
        @pl.when(i + 1 < block // group)
        def _():
            fetch(i + 1).start()

        fetch(i).wait()
        rows_done = attend_rows(group, i * group, lengths, queries, kv_buf.at[i % 2])
        by_head = jnp.swapaxes(rows_done, 0, 1)
        at = rows_of(((i // steps) * nt + t) * steps + i % steps, group)
        for h in range(by_head.shape[0]):
            full[at, h * HD : (h + 1) * HD] = by_head[h].astype(jnp.bfloat16)

        @pl.when(i == 0)
        def _():
            weight_copy.start()

        return carry

    def send_piece(j):
        for k in range(1, nt // 2):
            across(k, j).start()
        beside(0, j).start()

    def wait_piece(j):
        for k in range(nt // 2):
            beside(k, j).wait_recv()

    lax.fori_loop(0, steps, attend_step, 0)
    send_piece(0)
    relay(0)
    weight_copy.wait()
    wait_piece(0)

    def shrink(j):
        at = slice(j * half, (j + 1) * half)
        part = jnp.dot(full[at, :], down[...], preferred_element_type=jnp.float32)
        rank = np_ * up_mine.shape[1]
        lane_slot = lax.broadcasted_iota(jnp.int32, (piece, part.shape[1]), 1) // rank
        lane_slot = lane_slot + t * (part.shape[1] // rank)
        part = jnp.concatenate(
            [
                jnp.where(lane_slot == slots[b], part[b * piece : (b + 1) * piece], 0.0)
                for b in range(rows // BLK)
            ],
            axis=0,
        ).astype(jnp.bfloat16)
        for q in range(np_):
            shr[q, j * part_share : (j + 1) * part_share, :] = part[q * part_share : (q + 1) * part_share]

    def hop(way, q, c):
        to = p + 1 if way == 0 else p - 1
        to = jnp.clip(to, 0, np_ - 1)
        return copy(
            outbox.at[way, q, c], inbox.at[way, q, c],
            hop_send.at[way, q, c], hop_recv.at[way, q, c], pool=to,
        )

    turns = PIECES * chunks
    busy = min(2, chunks)

    def hops(c):
        behind = (p, np_ - 1 - p)
        for k in range(np_):
            for way in (0, 1):
                q = np_ - 1 - k if way == 0 else k
                ahead = (q > p) if way == 0 else (q < p)
                at = c - behind[way]
                inside = (at >= 0) & (at < turns)
                d = jnp.clip(at, 0, turns - 1)
                cols = pl.ds(pl.multiple_of(d % chunks * wide, wide), wide)
                lines = rows_of(d // chunks * np_ + q, part_share)

                @pl.when(inside & ahead & (behind[way] == 0))
                def _():
                    outbox[way, q, d] = total[lines, cols].astype(jnp.bfloat16)
                    hop(way, q, d).start()

                @pl.when(inside & ahead & (behind[way] > 0))
                def _():
                    hop(way, q, d).wait_recv()
                    part = total[lines, cols] + inbox[way, q, d].astype(jnp.float32)
                    outbox[way, q, d] = part.astype(jnp.bfloat16)
                    hop(way, q, d).start()

                @pl.when(inside & (p == q) & (behind[way] > 0))
                def _():
                    hop(way, q, d).wait_recv()
                    total[lines, cols] = total[lines, cols] + inbox[way, q, d].astype(jnp.float32)

    def one(k):
        q = (p + k) % np_
        return copy(shr.at[q], shr_in.at[k], one_send.at[k], one_recv.at[k], pool=q)

    def two(k):
        return copy(shr_sum, shr_peer.at[k], two_send.at[k], two_recv.at[k], tensor=(t + k) % nt)

    def step(c, carry):
        @pl.when(c == chunks)
        def _():
            wait_piece(1)

        @pl.when(c < turns)
        def _():
            cols = pl.ds(pl.multiple_of(c % chunks * wide, wide), wide)
            lines = rows_of(c // chunks, half)
            total[lines, cols] = jnp.dot(
                full[lines, :], weight[:, cols], preferred_element_type=jnp.float32
            )

        hops(c)

        @pl.when(c < busy)
        def _():
            each = steps // busy
            lax.fori_loop(steps + c * each, steps + (c + 1) * each, attend_step, 0)

        @pl.when(c == busy - 1)
        def _():
            send_piece(1)

        @pl.when(c == chunks - 1)
        def _():
            shrink(0)
            relay(1)

        @pl.when(c == chunks)
        def _():
            shrink(1)
            for k in range(1, np_):
                one(k).start()

        @pl.when(c == turns)
        def _():
            summed = shr[p].astype(jnp.float32)
            for k in range(1, np_):
                one(k).wait_recv()
                summed = summed + shr_in[k].astype(jnp.float32)
            shr_sum[...] = summed.astype(jnp.bfloat16)
            for k in range(1, nt):
                two(k).start()

        return carry

    lax.fori_loop(0, turns + np_ - 1, step, 0)

    halves = shr_sum[...].astype(jnp.float32)
    for k in range(1, nt):
        two(k).wait_recv()
        halves = halves + shr_peer[k].astype(jnp.float32)
    rank = np_ * up_mine.shape[1]
    ranks = halves[:, :rank]
    for k in range(1, halves.shape[1] // rank):
        ranks = ranks + halves[:, k * rank : (k + 1) * rank]
    shr_sum_rows = ranks.astype(jnp.bfloat16)
    ups[0] = up_mine[pl.ds(p * per_share, per_share)]
    for k in range(1, np_):
        q = (p + k) % np_
        copy(up_mine.at[pl.ds(q * per_share, per_share)], ups.at[k], up_send.at[k], up_recv.at[k], pool=q).wait_recv()
    for i in range(per_share):
        order = [ups[(p - z + np_) % np_, i].astype(jnp.float32) for z in range(np_)]
        up = jnp.concatenate(order, axis=0).astype(jnp.bfloat16)
        for j in range(PIECES):
            first = j * part_share + i * piece
            expand = jnp.dot(
                shr_sum_rows[first : first + piece], up, preferred_element_type=jnp.float32
            )
            at = rows_of(j * (half // piece) + p * per_share + i, piece)
            to = i * BLK + j * piece
            out[to : to + piece, :] = (total[at, :] + adapter_scale * expand).astype(jnp.bfloat16)

    for each in sends:
        each.wait_send()
    for j in range(PIECES):
        for k in range(nt // 2):
            beside(k, j).wait_send()
        for k in range(1, nt // 2):
            across(k, j).wait_send()
    for k in range(1, np_):
        one(k).wait_send()
    for k in range(1, nt):
        two(k).wait_send()

    def drain(c, carry):
        for q in range(np_):
            for way in (0, 1):
                ahead = (q > p) if way == 0 else (q < p)

                @pl.when(ahead)
                def _():
                    hop(way, q, c).wait_send()

        return carry

    lax.fori_loop(0, turns, drain, 0)


def make_local(nt, np_):
    def local(
        queries,
        key_value_cache,
        cache_lengths,
        block_adapter_slot,
        output_weight,
        adapter_down_weight,
        adapter_up_weight,
    ):
        block, feat = queries.shape
        rows = block * nt
        share = rows // np_
        slots, _, rank = adapter_down_weight.shape
        columns = output_weight.shape[1]
        chunks = max(1, min(4, columns // 512))
        wide = columns // chunks
        lanes = slots * rank
        down = jnp.transpose(adapter_down_weight, (1, 0, 2)).reshape(feat, lanes)
        per_share = share // BLK
        bf = jnp.bfloat16
        dma = pltpu.SemaphoreType.DMA
        boxes = (2, np_, PIECES * chunks, share // PIECES, wide)
        return pl.pallas_call(
            functools.partial(project_kernel, nt, np_, chunks),
            out_shape=jax.ShapeDtypeStruct((share, columns), bf),
            in_specs=[
                pl.BlockSpec(memory_space=pltpu.SMEM),
                pl.BlockSpec(memory_space=pltpu.VMEM),
                pl.BlockSpec(memory_space=pl.ANY),
                pl.BlockSpec(memory_space=pl.ANY),
            ]
            + [
                pl.BlockSpec(memory_space=pltpu.VMEM),
                pl.BlockSpec(memory_space=pltpu.SMEM),
                pl.BlockSpec(memory_space=pltpu.VMEM),
            ],
            out_specs=pl.BlockSpec(memory_space=pltpu.VMEM),
            scratch_shapes=[
                pltpu.VMEM((rows // BLK,) + adapter_up_weight.shape[1:], bf),
                pltpu.VMEM((2, STEP) + key_value_cache.shape[1:], bf),
                dma((2,)),
                pltpu.VMEM((feat, columns), bf),
                dma,
                pltpu.VMEM((rows, feat), bf),
                pltpu.VMEM((rows, columns), jnp.float32),
                pltpu.VMEM(boxes, bf),
                pltpu.VMEM(boxes, bf),
                pltpu.VMEM((np_, per_share, adapter_up_weight.shape[1], columns), bf),
                pltpu.VMEM((np_, share, lanes), bf),
                pltpu.VMEM((np_, share, lanes), bf),
                pltpu.VMEM((share, lanes), bf),
                pltpu.VMEM((nt, share, lanes), bf),
                dma((nt // 2, PIECES)), dma((nt // 2, PIECES)), dma((nt // 2, PIECES)), dma((nt // 2, PIECES)),
                dma((2, np_, PIECES * chunks)), dma((2, np_, PIECES * chunks)),
                dma((np_,)), dma((np_,)), dma((np_,)), dma((np_,)),
                dma((nt,)), dma((nt,)),
            ],
            compiler_params=pltpu.CompilerParams(
                collective_id=0, has_side_effects=True, vmem_limit_bytes=50 * 1024 * 1024
            ),
            cost_estimate=pl.CostEstimate(
                flops=2 * rows * feat * columns, bytes_accessed=2 * feat * columns, transcendentals=0
            ),
        )(
            cache_lengths, queries.reshape(block, feat // HD, HD), key_value_cache, output_weight,
            down, block_adapter_slot, adapter_up_weight,
        )

    return local


def solution(mesh):
    in_specs = (
        P(("groups", "tensor"), "pool"),
        P(("groups", "tensor"), None, None, "pool"),
        P(("groups", "tensor")),
        P("groups"),
        P("pool", "tensor"),
        P(("groups", "tensor"), "pool", None),
        P("groups", "pool", "tensor"),
    )
    out_specs = P(("groups", "pool"), "tensor")
    return jax.shard_map(make_local(mesh.shape["tensor"], mesh.shape["pool"]), mesh=mesh, in_specs=in_specs, out_specs=out_specs, check_vma=False)
```
